32 devices in a mesh: groups: 2 (over x), scene: 16 (over z, y, core).
Axes of the slice: x: 2, y: 2, z: 4, core: 2. Of those that a mesh axis runs over, the one named last changes fastest.
Arguments:
- tokens: bfloat16 [32, 196, 768], P(('groups', 'scene')), parts along dimension 0, may hold values from -6 to 6
- qkv_weight: bfloat16 [768, 2304], replicated, may hold values from -0.21875 to 0.21875
- out_weight: bfloat16 [768, 768], replicated, may hold values from -0.21875 to 0.21875
- attn_gain: float32 [768], replicated, may hold values from 0.1 to 1.9
- head_gain: float32 [768], replicated, may hold values from 0.1 to 1.9
- head_weight: bfloat16 [768, 1024], replicated, may hold values from -0.21875 to 0.21875
- head_bias: float32 [1024], replicated, may hold values from -3 to 3
- pair_list: int32 [64, 2], P('groups'), parts along dimension 0, may hold values from 0 to 15, as said below
- pair_count: int32 [32], P('groups'), parts along dimension 0, may hold values from 1 to 2, as said below
Outputs:
- joined: float32 [32, 196, 768], P(('groups', 'scene')), parts along dimension 0
The draws below stay inside these ranges and needn't reach their ends.
There are 2 independent parts, one for each index of `groups`. The reference program is written for one: setup_inputs(seed, part) draws one part's arguments, and reference() takes and returns one part's arrays. A program takes and returns all parts, laid end to end along the dimension named above; an argument that names none is the same for every part. Nothing has to cross between parts.
Inputs may be any that keep to these rules, and one draw needn't show every extreme that they name: `pair_list`: slot j of device d (row d * 2 + j) holds a pair whose first image is d + (j mod 1); its second image is owned by a device 1 to 2 places away along the scene axis taken as a cycle, image i being owned by device i. `pair_count`: entry d is the number of live slots of device d; slots from that number on are ignored. In every draw some device has exactly 2 and another exactly 1.
All inputs are finite; a program needn't handle non-finite values.
Results may differ from the reference program's by a relative error of at most 0.0045.
Values may be sent and summed in bfloat16 or wider, within the bound.
A program may use at most 128 MiB of HBM per device.

```python
import jax
import jax.numpy as jnp
from jax import lax

D = 768
HEADS = 12
TOK = 196
PM = 1024
IMG_DEV = 1
PAIR_DEV = 2
REACH = 2
IMAGES = 16
PAIRS = 32


def draw_pair_list(key, part):
    slot_index = jnp.arange(PAIRS, dtype=jnp.int32)
    device = slot_index // PAIR_DEV
    first_image = device * IMG_DEV + slot_index % PAIR_DEV % IMG_DEV
    key_a, key_b, key_c = jax.random.split(jax.random.fold_in(key, 11), 3)
    distance = jax.random.randint(key_a, (PAIRS,), 1, REACH + 1, dtype=jnp.int32)
    direction = jax.random.randint(key_b, (PAIRS,), 0, 2, dtype=jnp.int32) * 2 - 1
    member = jax.random.randint(key_c, (PAIRS,), 0, IMG_DEV, dtype=jnp.int32)
    devices = PAIRS // PAIR_DEV
    other_device = (device + direction * distance) % devices
    second_image = other_device * IMG_DEV + member
    return jnp.stack([first_image, second_image], axis=1).astype(jnp.int32)


def draw_pair_count(key, part):
    devices = PAIRS // PAIR_DEV
    key_a, key_b, key_c, key_d = jax.random.split(jax.random.fold_in(key, 23), 4)
    first_draw = jax.random.randint(key_a, (devices,), IMG_DEV, PAIR_DEV + 1, dtype=jnp.int32)
    second_draw = jax.random.randint(key_d, (devices,), IMG_DEV, PAIR_DEV + 1, dtype=jnp.int32)
    counts = jnp.minimum(first_draw, second_draw)
    highest = jax.random.randint(key_b, (), 0, devices, dtype=jnp.int32)
    lowest = (highest + 1 + jax.random.randint(key_c, (), 0, devices - 1, dtype=jnp.int32)) % devices
    positions = jnp.arange(devices, dtype=jnp.int32)
    counts = jnp.where(positions == highest, PAIR_DEV, counts)
    counts = jnp.where(positions == lowest, IMG_DEV, counts)
    return counts.astype(jnp.int32)


def block_scale(own_key, dims, cuts, low, high):
    gain, own = 1.0, jax.random.fold_in(own_key, 6)
    for axis_at, parts in cuts:
        steps = jnp.exp(jax.random.uniform(jax.random.fold_in(own, axis_at), (parts,), jnp.float32, low / len(cuts), high / len(cuts)))
        gain = gain * jnp.repeat(steps, dims[axis_at] // parts).reshape([-1 if axis == axis_at else 1 for axis in range(len(dims))])
    return gain


def noise(rng, extent, scale, limit, cuts=(), kind=jnp.bfloat16):
    array = jax.random.normal(rng, extent, jnp.float32) * scale
    if len(cuts) > 0:
        array = block_scale(rng, extent, cuts, -0.22, 0.18) * array
    return jnp.clip(array, min=-limit, max=limit).astype(kind)


def setup_inputs(seed: int = 0, part: int = 0) -> dict:
    key_list = jax.random.split(jax.random.key(seed), 10)
    part_splits = jax.random.split(jax.random.fold_in(key_list[9], part), 10)
    tokens = noise(part_splits[0], (IMAGES, TOK, D), 1.0, 6.0, ((0, 16),))
    qkv_weight = noise(key_list[1], (D, 3 * D), D ** -0.5, 0.21875)
    out_weight = noise(key_list[2], (D, D), D ** -0.5, 0.21875)
    attn_gain = jnp.clip(1.0 + 0.18 * jax.random.normal(key_list[3], (D,), jnp.float32), 0.1, 1.9)
    head_gain = jnp.clip(1.0 + 0.18 * jax.random.normal(key_list[4], (D,), jnp.float32), 0.1, 1.9)
    head_weight = noise(key_list[5], (D, PM), D ** -0.5, 0.21875)
    head_bias = noise(key_list[6], (PM,), 0.5, 3.0, (), jnp.float32)
    pair_list = draw_pair_list(jax.random.fold_in(jax.random.fold_in(key_list[9], part), 71), part)
    pair_count = draw_pair_count(jax.random.fold_in(jax.random.fold_in(key_list[9], part), 71), part)
    return {"tokens": tokens, "qkv_weight": qkv_weight, "out_weight": out_weight, "attn_gain": attn_gain, "head_gain": head_gain, "head_weight": head_weight, "head_bias": head_bias, "pair_list": pair_list, "pair_count": pair_count}


TEMPER = 16.0
CONF_RANGE = 4.0
EPSILON = 1e-06

def layer_norm(values, gain_vec):
    centred = values - lax.optimization_barrier(jnp.mean(values, axis=-1, keepdims=True))
    spread = lax.optimization_barrier(jnp.mean(centred * centred, axis=-1, keepdims=True))
    return centred * lax.rsqrt(spread + EPSILON) * gain_vec

def head_unit(values):
    shaped = values.reshape(values.shape[:-1] + (HEADS, values.shape[-1] // HEADS))
    energy = lax.optimization_barrier(jnp.mean(shaped * shaped, axis=-1, keepdims=True))
    return (shaped * lax.rsqrt(energy + EPSILON)).reshape(values.shape)

def project(single_image, attn_gain, qkv_weight):
    model_width = single_image.shape[-1]
    normed = layer_norm(single_image.astype(jnp.float32), attn_gain.astype(jnp.float32)).astype(jnp.bfloat16)
    mixed = jnp.dot(normed, qkv_weight, preferred_element_type=jnp.float32)
    queries = head_unit(mixed[:, :model_width]).astype(jnp.bfloat16)
    key_rows = head_unit(mixed[:, model_width:2 * model_width]).astype(jnp.bfloat16)
    values = mixed[:, 2 * model_width:].astype(jnp.bfloat16)
    return (queries, key_rows, values)

def view_maps(own_rows, queries, key_rows, values, out_weight, head_gain, head_weight, head_bias):
    view_count, token_count, model_width = own_rows.shape
    head_size = model_width // HEADS
    query_heads = queries.astype(jnp.float32).reshape(view_count, token_count, HEADS, head_size)
    key_heads = key_rows.astype(jnp.float32).reshape(view_count, token_count, HEADS, head_size)
    value_heads = values.astype(jnp.float32).reshape(view_count, token_count, HEADS, head_size)
    scores = jnp.einsum('vthc,vshc->vhts', query_heads, key_heads) * (TEMPER / head_size)
    exponent = jnp.exp(scores)
    attention = (exponent / lax.optimization_barrier(jnp.sum(exponent, axis=-1, keepdims=True))).astype(jnp.bfloat16)
    attended = jnp.einsum('vhts,vshc->vthc', attention.astype(jnp.float32), value_heads)
    attended = attended.reshape(view_count, token_count, model_width).astype(jnp.bfloat16)
    mixed = own_rows.astype(jnp.float32) + jnp.einsum('vtd,de->vte', attended.astype(jnp.float32), out_weight.astype(jnp.float32))
    head_in = layer_norm(mixed, head_gain.astype(jnp.float32)).astype(jnp.bfloat16)
    head_out = jnp.einsum('vtd,de->vte', head_in.astype(jnp.float32), head_weight.astype(jnp.float32)) + head_bias.astype(jnp.float32)
    xyz_cols = 3 * (head_weight.shape[1] // 4)
    return (head_out[..., :xyz_cols].astype(jnp.bfloat16), head_out[..., xyz_cols:].astype(jnp.bfloat16))

def reference(tokens, qkv_weight, out_weight, attn_gain, head_gain, head_weight, head_bias, pair_list, pair_count):
    all_queries, all_keys, all_values = lax.map(lambda single_image: project(single_image, attn_gain, qkv_weight), tokens)
    pixels = head_weight.shape[1] // 4
    image_count, token_count, model_width = tokens.shape

    def add_pair(totals, slot_index):
        weighted_sum, weight_sum = totals
        pair_rows = pair_list[slot_index]
        partner_ids = pair_rows[::-1]
        device = slot_index // PAIR_DEV
        live_flag = (slot_index % PAIR_DEV < pair_count[device]).astype(jnp.float32)
        xyz, conf = view_maps(tokens[pair_rows], all_queries[pair_rows], all_keys[partner_ids], all_values[partner_ids], out_weight, head_gain, head_weight, head_bias)
        weight = jnp.exp(CONF_RANGE * jnp.tanh(conf.astype(jnp.float32) / CONF_RANGE)) * live_flag
        weighted = (weight[:, :, None, :] * xyz.astype(jnp.float32).reshape(2, token_count, 3, pixels)).reshape(2, token_count, 3 * pixels)
        weighted_sum = weighted_sum.at[pair_rows].add(weighted)
        weight_sum = weight_sum.at[pair_rows].add(weight)
        return ((weighted_sum, weight_sum), None)
    start = (jnp.zeros((image_count, token_count, 3 * pixels), jnp.float32), jnp.zeros((image_count, token_count, pixels), jnp.float32))
    (weighted_sum, weight_sum), _ = lax.scan(add_pair, start, jnp.arange(pair_list.shape[0], dtype=jnp.int32))
    return weighted_sum / jnp.tile(weight_sum, (1, 1, 3))
```

```python
import functools

import jax
import jax.numpy as jnp
from jax import lax
from jax.experimental import pallas as pl
from jax.experimental.pallas import tpu as pltpu
from jax.sharding import PartitionSpec as P

HEADS = 12
TEMPER = 16.0
CONF_RANGE = 4.0
EPSILON = 1e-06
F32 = jnp.float32
BF16 = jnp.bfloat16
MATE, AHEAD, BEHIND, RELAYED = range(4)


def layer_norm(values, gain_row):
    centred = values - jnp.mean(values, axis=-1, keepdims=True)
    spread = jnp.mean(centred * centred, axis=-1, keepdims=True)
    return centred * lax.rsqrt(spread + EPSILON) * gain_row


def product(left, right):
    return jnp.dot(left, right, preferred_element_type=F32)


def scene_kernel(
    n,
    tokens_ref,
    attn_gain_ref,
    head_gain_ref,
    head_bias_ref,
    pairs_ref,
    count_ref,
    qkv_hbm,
    out_hbm,
    head_hbm,
    joined_ref,
    qkv_ref,
    outw_ref,
    headw_ref,
    rows_ref,
    own_ref,
    recv_ref,
    query_ref,
    attended_ref,
    sum_ref,
    weight_ref,
    load_sem,
    send_sem,
    recv_sem,
):
    token_count, width = tokens_ref.shape[1:]
    padded = rows_ref.shape[0]
    head = width // HEADS
    pair = 2 * head
    group = 2 * pair
    pixels = headw_ref.shape[1] // 4
    slots = pairs_ref.shape[1] // n

    me = lax.axis_index("scene")
    sign = 1 - 2 * lax.rem(me, 2)

    def at(steps):
        return lax.rem(me + steps * sign + n, n)

    loads = [
        pltpu.make_async_copy(source, target, load_sem.at[k])
        for k, (source, target) in enumerate(
            ((qkv_hbm, qkv_ref), (out_hbm, outw_ref), (head_hbm, headw_ref))
        )
    ]
    barrier = pltpu.get_barrier_semaphore()
    for steps in (1, 2, -2):
        pl.semaphore_signal(barrier, inc=1, device_id={"scene": at(steps)})
    for load in loads:
        load.start()

    rows_ref[...] = jnp.zeros_like(rows_ref)
    rows_ref[0:token_count] = tokens_ref[0].astype(F32)
    own_ref[...] = layer_norm(rows_ref[...], attn_gain_ref[...]).astype(BF16)
    pl.semaphore_wait(barrier, 3)

    def send(source, slot, steps):
        copy = pltpu.make_async_remote_copy(
            src_ref=source,
            dst_ref=recv_ref.at[slot],
            send_sem=send_sem.at[slot],
            recv_sem=recv_sem.at[slot],
            device_id={"scene": at(steps)},
        )
        copy.start()
        return copy

    copies = {}
    copies[AHEAD] = send(own_ref, AHEAD, -2)
    copies[BEHIND] = send(own_ref, BEHIND, 2)
    copies[MATE] = send(own_ref, MATE, 1)

    across = lax.broadcasted_iota(jnp.int32, (group, group), 0) // head
    along = lax.broadcasted_iota(jnp.int32, (group, group), 1) // head
    same_head = jnp.where(across == along, 1.0 / head, 0.0).astype(BF16)
    first_head = lax.broadcasted_iota(jnp.int32, (padded, pair), 1) < head
    ones = jnp.where(
        lax.broadcasted_iota(jnp.int32, (padded, pair), 0) < token_count, 1.0, 0.0
    ).astype(BF16)

    def unit(mixed):
        energy = product((mixed * mixed).astype(BF16), same_head)
        return mixed * lax.rsqrt(energy + EPSILON)

    loads[0].wait()
    for g in range(width // group):
        queries = unit(product(own_ref[...], qkv_ref[:, g * group : (g + 1) * group]))
        queries = queries * (TEMPER / head)
        for h in range(2):
            block = queries[:, h * pair : (h + 1) * pair]
            query_ref[2 * g + h, 0:padded] = jnp.where(first_head, block, 0.0).astype(BF16)
            query_ref[2 * g + h, padded : 2 * padded] = jnp.where(
                first_head, 0.0, block
            ).astype(BF16)

    def multiplicity(steps):
        other = at(steps)
        total = jnp.float32(0.0)
        for owner, partner in ((me, other), (other, me)):
            for k in range(slots):
                hit = (pairs_ref[1, owner * slots + k] == partner) & (k < count_ref[owner])
                total = total + jnp.where(hit, 1.0, 0.0)
        return total

    def view(slot, steps, first):
        partner = recv_ref[slot]
        for g in range(width // group):
            low = width + g * group
            keys = unit(product(partner, qkv_ref[:, low : low + group])).astype(BF16)
            values = product(
                partner, qkv_ref[:, low + width : low + width + group]
            ).astype(BF16)
            for h in range(2):
                cols = slice(h * pair, (h + 1) * pair)
                scores = lax.dot_general(
                    query_ref[2 * g + h],
                    keys[:, cols],
                    (((1,), (1,)), ((), ())),
                    preferred_element_type=F32,
                )
                mixed = product(
                    jnp.exp(scores).astype(BF16),
                    jnp.concatenate([values[:, cols], ones], axis=1),
                )
                top, bottom = mixed[:padded], mixed[padded:]
                attended_ref[:, g * group + h * pair : g * group + (h + 1) * pair] = (
                    jnp.where(first_head, top[:, :pair], bottom[:, :pair])
                    / jnp.where(first_head, top[:, pair:], bottom[:, pair:])
                ).astype(BF16)
        if first:
            loads[1].wait()
            loads[2].wait()
        mixed = rows_ref[...] + product(attended_ref[...], outw_ref[...])
        head_in = layer_norm(mixed, head_gain_ref[...]).astype(BF16)

        def head_cols(c):
            cols = slice(c * pixels, (c + 1) * pixels)
            made = product(head_in, headw_ref[:, cols]) + head_bias_ref[:, cols]
            return made.astype(BF16).astype(F32)

        weight = jnp.exp(CONF_RANGE * jnp.tanh(head_cols(3) / CONF_RANGE)) * multiplicity(steps)
        weight_ref[...] = weight if first else weight_ref[...] + weight
        for c in range(3):
            cols = slice(c * pixels, (c + 1) * pixels)
            part = weight * head_cols(c)
            sum_ref[:, cols] = part if first else sum_ref[:, cols] + part

    copies[MATE].wait_recv()
    view(MATE, 1, True)
    copies[AHEAD].wait_recv()
    copies[RELAYED] = send(recv_ref.at[AHEAD], RELAYED, 1)
    view(AHEAD, 2, False)
    copies[BEHIND].wait_recv()
    view(BEHIND, -2, False)
    copies[RELAYED].wait_recv()
    view(RELAYED, -1, False)

    for c in range(3):
        cols = slice(c * pixels, (c + 1) * pixels)
        joined_ref[0, :, cols] = (sum_ref[:, cols] / weight_ref[...])[:token_count]
    for slot in range(4):
        copies[slot].wait_send()


def per_device(
    n,
    tokens,
    qkv_weight,
    out_weight,
    attn_gain,
    head_gain,
    head_weight,
    head_bias,
    pair_list,
    pair_count,
):
    _, token_count, width = tokens.shape
    padded = -(-token_count // 16) * 16
    pixels = head_weight.shape[1] // 4
    vmem = pl.BlockSpec(memory_space=pltpu.VMEM)
    smem = pl.BlockSpec(memory_space=pltpu.SMEM)
    hbm = pl.BlockSpec(memory_space=pl.ANY)
    return pl.pallas_call(
        functools.partial(scene_kernel, n),
        out_shape=jax.ShapeDtypeStruct(tokens.shape, F32),
        in_specs=[vmem] * 4 + [smem] * 2 + [hbm] * 3,
        out_specs=vmem,
        scratch_shapes=[
            pltpu.VMEM(qkv_weight.shape, BF16),
            pltpu.VMEM(out_weight.shape, BF16),
            pltpu.VMEM(head_weight.shape, BF16),
            pltpu.VMEM((padded, width), F32),
            pltpu.VMEM((padded, width), BF16),
            pltpu.VMEM((4, padded, width), BF16),
            pltpu.VMEM((HEADS // 2, 2 * padded, 2 * width // HEADS), BF16),
            pltpu.VMEM((padded, width), BF16),
            pltpu.VMEM((padded, 3 * pixels), F32),
            pltpu.VMEM((padded, pixels), F32),
            pltpu.SemaphoreType.DMA((3,)),
            pltpu.SemaphoreType.DMA((4,)),
            pltpu.SemaphoreType.DMA((4,)),
        ],
        compiler_params=pltpu.CompilerParams(
            collective_id=0, has_side_effects=True, vmem_limit_bytes=60 * 2**20
        ),
        name="scene",
    )(
        tokens,
        attn_gain[None],
        head_gain[None],
        head_bias[None],
        pair_list.T,
        pair_count,
        qkv_weight,
        out_weight,
        head_weight,
    )


def solution(mesh):
    return jax.shard_map(
        functools.partial(per_device, mesh.shape["scene"]),
        mesh=mesh,
        in_specs=(
            P(("groups", "scene"), None, None),
            P(),
            P(),
            P(),
            P(),
            P(),
            P(),
            P("groups", None),
            P("groups"),
        ),
        out_specs=P(("groups", "scene"), None, None),
        check_vma=False,
    )
```

```python
import functools

import jax
import jax.numpy as jnp
from jax import lax
from jax.experimental import pallas as pl
from jax.experimental.pallas import tpu as pltpu
from jax.sharding import PartitionSpec as P

HEADS = 12
TEMPER = 16.0
CONF_RANGE = 4.0
EPSILON = 1e-06
F32 = jnp.float32
BF16 = jnp.bfloat16
MATE, AHEAD, BEHIND, RELAYED = range(4)


def layer_norm(values, gain_row):
    centred = values - jnp.mean(values, axis=-1, keepdims=True)
    spread = jnp.mean(centred * centred, axis=-1, keepdims=True)
    return centred * lax.rsqrt(spread + EPSILON) * gain_row[None]


def product(left, right):
    return jnp.dot(left, right, preferred_element_type=F32)


def scene_kernel(
    n,
    tokens_ref,
    attn_gain_ref,
    head_gain_ref,
    head_bias_ref,
    pairs_ref,
    count_ref,
    qkv_hbm,
    out_hbm,
    head_hbm,
    joined_ref,
    qkv_ref,
    outw_ref,
    headw_ref,
    rows_ref,
    own_ref,
    recv_ref,
    query_ref,
    attended_ref,
    sum_ref,
    weight_ref,
    load_sem,
    send_sem,
    recv_sem,
):
    token_count, width = tokens_ref.shape[1:]
    padded = rows_ref.shape[0]
    head = width // HEADS
    pair = 2 * head
    group = 2 * pair
    pixels = headw_ref.shape[1] // 4
    slots = pairs_ref.shape[1] // n

    me = lax.axis_index("scene")
    sign = 1 - 2 * lax.rem(me, 2)

    def at(steps):
        return lax.rem(me + steps * sign + n, n)

    loads = [
        pltpu.make_async_copy(source, target, load_sem.at[k])
        for k, (source, target) in enumerate(
            ((qkv_hbm, qkv_ref), (out_hbm, outw_ref), (head_hbm, headw_ref))
        )
    ]
    barrier = pltpu.get_barrier_semaphore()
    for steps in (1, 2, -2):
        pl.semaphore_signal(barrier, inc=1, device_id={"scene": at(steps)})
    for load in loads:
        load.start()

    rows_ref[...] = jnp.zeros_like(rows_ref)
    rows_ref[0:token_count] = tokens_ref[0].astype(F32)
    own_ref[...] = layer_norm(rows_ref[...], attn_gain_ref[...]).astype(BF16)
    pl.semaphore_wait(barrier, 3)

    def send(source, slot, steps):
        copy = pltpu.make_async_remote_copy(
            src_ref=source,
            dst_ref=recv_ref.at[slot],
            send_sem=send_sem.at[slot],
            recv_sem=recv_sem.at[slot],
            device_id={"scene": at(steps)},
        )
        copy.start()
        return copy

    copies = {}
    copies[MATE] = send(own_ref, MATE, 1)
    copies[AHEAD] = send(own_ref, AHEAD, -2)

    across = lax.broadcasted_iota(jnp.int32, (group, group), 0) // head
    along = lax.broadcasted_iota(jnp.int32, (group, group), 1) // head
    same_head = jnp.where(across == along, 1.0 / head, 0.0).astype(BF16)
    first_head = lax.broadcasted_iota(jnp.int32, (padded, pair), 1) < head
    ones = jnp.where(
        lax.broadcasted_iota(jnp.int32, (padded, pair), 0) < token_count, 1.0, 0.0
    ).astype(BF16)

    def unit(mixed):
        energy = product((mixed * mixed).astype(BF16), same_head)
        return mixed * lax.rsqrt(energy + EPSILON)

    loads[0].wait()
    for g in range(width // group):
        queries = unit(product(own_ref[...], qkv_ref[:, g * group : (g + 1) * group]))
        queries = queries * (TEMPER / head)
        for h in range(2):
            block = queries[:, h * pair : (h + 1) * pair]
            query_ref[2 * g + h, 0:padded] = jnp.where(first_head, block, 0.0).astype(BF16)
            query_ref[2 * g + h, padded : 2 * padded] = jnp.where(
                first_head, 0.0, block
            ).astype(BF16)

    def multiplicity(steps):
        other = at(steps)
        total = jnp.float32(0.0)
        for owner, partner in ((me, other), (other, me)):
            for k in range(slots):
                hit = (pairs_ref[1, owner * slots + k] == partner) & (k < count_ref[owner])
                total = total + jnp.where(hit, 1.0, 0.0)
        return total

    def view(slot, steps, first):
        partner = recv_ref[slot]
        for g in range(width // group):
            low = width + g * group
            keys = unit(product(partner, qkv_ref[:, low : low + group])).astype(BF16)
            values = product(
                partner, qkv_ref[:, low + width : low + width + group]
            ).astype(BF16)
            for h in range(2):
                cols = slice(h * pair, (h + 1) * pair)
                scores = lax.dot_general(
                    query_ref[2 * g + h],
                    keys[:, cols],
                    (((1,), (1,)), ((), ())),
                    preferred_element_type=F32,
                )
                mixed = product(
                    jnp.exp(scores).astype(BF16),
                    jnp.concatenate([values[:, cols], ones], axis=1),
                )
                top, bottom = mixed[:padded], mixed[padded:]
                attended_ref[:, g * group + h * pair : g * group + (h + 1) * pair] = (
                    jnp.where(first_head, top[:, :pair], bottom[:, :pair])
                    / jnp.where(first_head, top[:, pair:], bottom[:, pair:])
                ).astype(BF16)
        if first:
            loads[1].wait()
            loads[2].wait()
        mixed = rows_ref[...] + product(attended_ref[...], outw_ref[...])
        head_in = layer_norm(mixed, head_gain_ref[...]).astype(BF16)

        def head_cols(c):
            cols = slice(c * pixels, (c + 1) * pixels)
            made = product(head_in, headw_ref[:, cols]) + head_bias_ref[:, cols]
            return made.astype(BF16).astype(F32)

        weight = jnp.exp(CONF_RANGE * jnp.tanh(head_cols(3) / CONF_RANGE)) * multiplicity(steps)
        weight_ref[...] = weight if first else weight_ref[...] + weight
        for c in range(3):
            cols = slice(c * pixels, (c + 1) * pixels)
            part = weight * head_cols(c)
            sum_ref[:, cols] = part if first else sum_ref[:, cols] + part

    copies[MATE].wait_recv()
    view(MATE, 1, True)
    copies[AHEAD].wait_send()
    copies[BEHIND] = send(own_ref, BEHIND, 2)
    copies[AHEAD].wait_recv()
    copies[RELAYED] = send(recv_ref.at[AHEAD], RELAYED, 1)
    view(AHEAD, 2, False)
    copies[RELAYED].wait_recv()
    view(RELAYED, -1, False)
    copies[BEHIND].wait_recv()
    view(BEHIND, -2, False)

    for c in range(3):
        cols = slice(c * pixels, (c + 1) * pixels)
        joined_ref[0, :, cols] = (sum_ref[:, cols] / weight_ref[...])[:token_count]
    for slot in (MATE, BEHIND, RELAYED):
        copies[slot].wait_send()


def per_device(
    n,
    tokens,
    qkv_weight,
    out_weight,
    attn_gain,
    head_gain,
    head_weight,
    head_bias,
    pair_list,
    pair_count,
):
    _, token_count, width = tokens.shape
    padded = -(-token_count // 16) * 16
    pixels = head_weight.shape[1] // 4
    vmem = pl.BlockSpec(memory_space=pltpu.VMEM)
    smem = pl.BlockSpec(memory_space=pltpu.SMEM)
    hbm = pl.BlockSpec(memory_space=pl.ANY)
    return pl.pallas_call(
        functools.partial(scene_kernel, n),
        out_shape=jax.ShapeDtypeStruct(tokens.shape, F32),
        in_specs=[vmem] * 4 + [smem] * 2 + [hbm] * 3,
        out_specs=vmem,
        scratch_shapes=[
            pltpu.VMEM(qkv_weight.shape, BF16),
            pltpu.VMEM(out_weight.shape, BF16),
            pltpu.VMEM(head_weight.shape, BF16),
            pltpu.VMEM((padded, width), F32),
            pltpu.VMEM((padded, width), BF16),
            pltpu.VMEM((4, padded, width), BF16),
            pltpu.VMEM((HEADS // 2, 2 * padded, 2 * width // HEADS), BF16),
            pltpu.VMEM((padded, width), BF16),
            pltpu.VMEM((padded, 3 * pixels), F32),
            pltpu.VMEM((padded, pixels), F32),
            pltpu.SemaphoreType.DMA((3,)),
            pltpu.SemaphoreType.DMA((4,)),
            pltpu.SemaphoreType.DMA((4,)),
        ],
        compiler_params=pltpu.CompilerParams(
            collective_id=0, has_side_effects=True, vmem_limit_bytes=60 * 2**20
        ),
        name="scene",
    )(
        tokens,
        attn_gain,
        head_gain,
        head_bias[None],
        pair_list.T,
        pair_count,
        qkv_weight,
        out_weight,
        head_weight,
    )


def solution(mesh):
    return jax.shard_map(
        functools.partial(per_device, mesh.shape["scene"]),
        mesh=mesh,
        in_specs=(
            P(("groups", "scene"), None, None),
            P(),
            P(),
            P(),
            P(),
            P(),
            P(),
            P("groups", None),
            P("groups"),
        ),
        out_specs=P(("groups", "scene"), None, None),
        check_vma=False,
    )
```

```python
import functools

import jax
import jax.numpy as jnp
from jax import lax
from jax.experimental import pallas as pl
from jax.experimental.pallas import tpu as pltpu
from jax.sharding import PartitionSpec as P

HEADS = 12
TEMPER = 16.0
CONF_RANGE = 4.0
EPSILON = 1e-06
F32 = jnp.float32
BF16 = jnp.bfloat16
MATE, AHEAD, BEHIND, RELAYED = range(4)


def layer_norm(values, gain_row):
    centred = values - jnp.mean(values, axis=-1, keepdims=True)
    spread = jnp.mean(centred * centred, axis=-1, keepdims=True)
    return centred * lax.rsqrt(spread + EPSILON) * gain_row[None]


def product(left, right):
    return jnp.dot(left, right, preferred_element_type=F32)


def scene_kernel(
    n,
    tokens_ref,
    attn_gain_ref,
    head_gain_ref,
    head_bias_ref,
    pairs_ref,
    count_ref,
    qkv_hbm,
    out_hbm,
    head_hbm,
    joined_ref,
    qkv_ref,
    outw_ref,
    headw_ref,
    rows_ref,
    own_ref,
    recv_ref,
    query_ref,
    attended_ref,
    sum_ref,
    weight_ref,
    load_sem,
    send_sem,
    recv_sem,
):
    token_count, width = tokens_ref.shape[1:]
    padded = rows_ref.shape[0]
    head = width // HEADS
    pair = 2 * head
    group = 2 * pair
    pixels = headw_ref.shape[1] // 4
    slots = pairs_ref.shape[1] // n

    me = lax.axis_index("scene")
    sign = 1 - 2 * lax.rem(me, 2)

    def at(steps):
        return lax.rem(me + steps * sign + n, n)

    loads = [
        pltpu.make_async_copy(source, target, load_sem.at[k])
        for k, (source, target) in enumerate(
            ((qkv_hbm, qkv_ref), (out_hbm, outw_ref), (head_hbm, headw_ref))
        )
    ]
    barrier = pltpu.get_barrier_semaphore()
    for steps in (1, 2, -2):
        pl.semaphore_signal(barrier, inc=1, device_id={"scene": at(steps)})
    loads[0].start()

    rows_ref[...] = jnp.zeros_like(rows_ref)
    rows_ref[0:token_count] = tokens_ref[0].astype(F32)
    own_ref[...] = layer_norm(rows_ref[...], attn_gain_ref[...]).astype(BF16)
    pl.semaphore_wait(barrier, 3)

    def send(source, slot, steps):
        copy = pltpu.make_async_remote_copy(
            src_ref=source,
            dst_ref=recv_ref.at[slot],
            send_sem=send_sem.at[slot],
            recv_sem=recv_sem.at[slot],
            device_id={"scene": at(steps)},
        )
        copy.start()
        return copy

    copies = {}
    copies[AHEAD] = send(own_ref, AHEAD, -2)
    copies[MATE] = send(own_ref, MATE, 1)
    for load in loads[1:]:
        load.start()

    across = lax.broadcasted_iota(jnp.int32, (group, group), 0) // head
    along = lax.broadcasted_iota(jnp.int32, (group, group), 1) // head
    same_head = jnp.where(across == along, 1.0 / head, 0.0).astype(BF16)
    first_head = lax.broadcasted_iota(jnp.int32, (padded, pair), 1) < head
    ones = jnp.where(
        lax.broadcasted_iota(jnp.int32, (padded, pair), 0) < token_count, 1.0, 0.0
    ).astype(BF16)

    def unit(mixed):
        energy = product((mixed * mixed).astype(BF16), same_head)
        return mixed * lax.rsqrt(energy + EPSILON)

    loads[0].wait()
    for g in range(width // group):
        queries = unit(product(own_ref[...], qkv_ref[:, g * group : (g + 1) * group]))
        queries = queries * (TEMPER / head)
        for h in range(2):
            block = queries[:, h * pair : (h + 1) * pair]
            query_ref[2 * g + h, 0:padded] = jnp.where(first_head, block, 0.0).astype(BF16)
            query_ref[2 * g + h, padded : 2 * padded] = jnp.where(
                first_head, 0.0, block
            ).astype(BF16)

    def multiplicity(steps):
        other = at(steps)
        total = jnp.float32(0.0)
        for owner, partner in ((me, other), (other, me)):
            for k in range(slots):
                hit = (pairs_ref[1, owner * slots + k] == partner) & (k < count_ref[owner])
                total = total + jnp.where(hit, 1.0, 0.0)
        return total

    def view(slot, steps, first):
        partner = recv_ref[slot]
        for g in range(width // group):
            low = width + g * group
            keys = unit(product(partner, qkv_ref[:, low : low + group])).astype(BF16)
            values = product(
                partner, qkv_ref[:, low + width : low + width + group]
            ).astype(BF16)
            for h in range(2):
                cols = slice(h * pair, (h + 1) * pair)
                scores = lax.dot_general(
                    query_ref[2 * g + h],
                    keys[:, cols],
                    (((1,), (1,)), ((), ())),
                    preferred_element_type=F32,
                )
                mixed = product(
                    jnp.exp(scores).astype(BF16),
                    jnp.concatenate([values[:, cols], ones], axis=1),
                )
                top, bottom = mixed[:padded], mixed[padded:]
                attended_ref[:, g * group + h * pair : g * group + (h + 1) * pair] = (
                    jnp.where(first_head, top[:, :pair], bottom[:, :pair])
                    / jnp.where(first_head, top[:, pair:], bottom[:, pair:])
                ).astype(BF16)
        if first:
            loads[1].wait()
            loads[2].wait()
        mixed = rows_ref[...] + product(attended_ref[...], outw_ref[...])
        head_in = layer_norm(mixed, head_gain_ref[...]).astype(BF16)

        def head_cols(c):
            cols = slice(c * pixels, (c + 1) * pixels)
            made = product(head_in, headw_ref[:, cols]) + head_bias_ref[:, cols]
            return made.astype(BF16).astype(F32)

        weight = jnp.exp(CONF_RANGE * jnp.tanh(head_cols(3) / CONF_RANGE)) * multiplicity(steps)
        weight_ref[...] = weight if first else weight_ref[...] + weight
        for c in range(3):
            cols = slice(c * pixels, (c + 1) * pixels)
            part = weight * head_cols(c)
            sum_ref[:, cols] = part if first else sum_ref[:, cols] + part

    copies[MATE].wait_recv()
    view(MATE, 1, True)
    copies[AHEAD].wait_send()
    copies[BEHIND] = send(own_ref, BEHIND, 2)
    copies[AHEAD].wait_recv()
    copies[RELAYED] = send(recv_ref.at[AHEAD], RELAYED, 1)
    view(AHEAD, 2, False)
    copies[RELAYED].wait_recv()
    view(RELAYED, -1, False)
    copies[BEHIND].wait_recv()
    view(BEHIND, -2, False)

    for c in range(3):
        cols = slice(c * pixels, (c + 1) * pixels)
        joined_ref[0, :, cols] = (sum_ref[:, cols] / weight_ref[...])[:token_count]
    for slot in (MATE, BEHIND, RELAYED):
        copies[slot].wait_send()


def per_device(
    n,
    tokens,
    qkv_weight,
    out_weight,
    attn_gain,
    head_gain,
    head_weight,
    head_bias,
    pair_list,
    pair_count,
):
    _, token_count, width = tokens.shape
    padded = -(-token_count // 16) * 16
    pixels = head_weight.shape[1] // 4
    vmem = pl.BlockSpec(memory_space=pltpu.VMEM)
    smem = pl.BlockSpec(memory_space=pltpu.SMEM)
    hbm = pl.BlockSpec(memory_space=pl.ANY)
    return pl.pallas_call(
        functools.partial(scene_kernel, n),
        out_shape=jax.ShapeDtypeStruct(tokens.shape, F32),
        in_specs=[vmem] * 4 + [smem] * 2 + [hbm] * 3,
        out_specs=vmem,
        scratch_shapes=[
            pltpu.VMEM(qkv_weight.shape, BF16),
            pltpu.VMEM(out_weight.shape, BF16),
            pltpu.VMEM(head_weight.shape, BF16),
            pltpu.VMEM((padded, width), F32),
            pltpu.VMEM((padded, width), BF16),
            pltpu.VMEM((4, padded, width), BF16),
            pltpu.VMEM((HEADS // 2, 2 * padded, 2 * width // HEADS), BF16),
            pltpu.VMEM((padded, width), BF16),
            pltpu.VMEM((padded, 3 * pixels), F32),
            pltpu.VMEM((padded, pixels), F32),
            pltpu.SemaphoreType.DMA((3,)),
            pltpu.SemaphoreType.DMA((4,)),
            pltpu.SemaphoreType.DMA((4,)),
        ],
        compiler_params=pltpu.CompilerParams(
            collective_id=0, has_side_effects=True, vmem_limit_bytes=60 * 2**20
        ),
        name="scene",
    )(
        tokens,
        attn_gain,
        head_gain,
        head_bias[None],
        pair_list.T,
        pair_count,
        qkv_weight,
        out_weight,
        head_weight,
    )


def solution(mesh):
    return jax.shard_map(
        functools.partial(per_device, mesh.shape["scene"]),
        mesh=mesh,
        in_specs=(
            P(("groups", "scene"), None, None),
            P(),
            P(),
            P(),
            P(),
            P(),
            P(),
            P("groups", None),
            P("groups"),
        ),
        out_specs=P(("groups", "scene"), None, None),
        check_vma=False,
    )
```
